128 devices in a mesh: fsdp: 32 (over y, z, x_hi), tenant: 4 (over x_lo, core).
Axes of the slice: x: 4 (x_hi: 2, x_lo: 2; x = x_hi * 2 + x_lo), y: 4, z: 4, core: 2. Of those that a mesh axis runs over, the one named last changes fastest.
Arguments:
- tokens: bfloat16 [32768, 16384], P(('fsdp', 'tenant'))
- cotangent: bfloat16 [32768, 16384], P(('fsdp', 'tenant')), may hold values from -6 to 6
- w_query: bfloat16 [16384, 256], P('fsdp'), may hold values from -0.046875 to 0.046875
- w_key: bfloat16 [16384, 128], P('fsdp'), may hold values from -0.046875 to 0.046875
- w_value: bfloat16 [16384, 128], P('fsdp'), may hold values from -0.046875 to 0.046875
- w_output: bfloat16 [256, 16384], P(None, 'fsdp'), may hold values from -0.375 to 0.375
- adapter_down: bfloat16 [16384, 8, 2, 16], P('fsdp', 'tenant'), may hold values from -0.046875 to 0.046875
- adapter_up: bfloat16 [8, 16, 384], P('tenant'), may hold values from -1.5 to 1.5
- tenant_slot: int32 [128], P(('fsdp', 'tenant')), may hold values from 0 to 1
- lengths: int32 [128], P(('fsdp', 'tenant')), may hold values from 1 to 256, as said below
Outputs:
- output: bfloat16 [32768, 16384], P(('fsdp', 'tenant'))
- grad_down: float32 [16384, 8, 2, 16], P('fsdp', 'tenant')
- grad_up: float32 [8, 16, 384], P('tenant')
The draws below stay inside these ranges and needn't reach their ends.
Inputs may be any that keep to these rules, and one draw needn't show every extreme that they name: `lengths`: sample 0 has all 256 tokens real; the others at least one.
All inputs are finite; a program needn't handle non-finite values.
Results may differ from the reference program's by a relative error of at most 0.0075.
The reference program's roundings to bfloat16 on the way count: a program that leaves them out, or rounds other values in their place, can miss the bound.
Values may be sent and summed in bfloat16 or wider, within the bound.
No kernel may reach another device: no remote copies, remote signals or barrier semaphores. Data moves between devices by JAX's collectives and lax.ppermute only.
A program may use at most 192 MiB of HBM per device.

```python
import jax
import jax.numpy as jnp
from jax import lax

D = 16384
HEAD_SIZE = 128
QH = 2
R = 16
TEN_DEV = 2
SEQ = 256
QUERY_FEATURES = 256
UPW = 384
TENANTS = 8
SAMPLES = 128
TOKENS = 32768
N_TENANT = 4


def draw_tokens(key, part):
    key = jax.random.fold_in(key, 11)
    first = jax.random.fold_in(key, 0)
    values = jnp.clip(jax.random.normal(first, (TOKENS, D), jnp.float32), -6.0, 6.0)
    return values.astype(jnp.bfloat16)


def draw_lengths(key, part):
    key = jax.random.fold_in(key, 23)
    drawn = jax.random.randint(key, (SAMPLES,), 1, SEQ + 1, dtype=jnp.int32)
    index = jnp.arange(SAMPLES, dtype=jnp.int32)
    return jnp.where(index == 0, jnp.int32(SEQ), drawn).astype(jnp.int32)


def with_ends(values, key, least, top_value):
    shape = values.shape
    index_at = [jax.random.randint(jax.random.fold_in(key, axis), (), 0, shape[axis]) for axis in range(len(shape))]
    values = values.at[tuple(index_at)].set(least)
    longest = shape.index(max(shape))
    index_at[longest] = (index_at[longest] + 1) % shape[longest]
    return values.at[tuple(index_at)].set(top_value)


def steps_of(stream_key, dims, cuts, least, top_value):
    def one(axis_at, blocks):
        steps = jax.random.uniform(jax.random.fold_in(jax.random.fold_in(stream_key, 6), axis_at), (blocks,), jnp.float32, least / len(cuts), top_value / len(cuts))
        return jnp.repeat(jnp.exp(steps), dims[axis_at] // blocks).reshape((-1,) + (1,) * (len(dims) - axis_at - 1))

    gain = one(*cuts[0])
    for cut in cuts[1:]:
        gain = gain * one(*cut)
    return gain


def scatter_about(own_key, extent, deviation, limit, cuts=(), kind=jnp.bfloat16):
    values = deviation * jax.random.normal(own_key, extent, jnp.float32)
    if cuts:
        values = values * steps_of(own_key, extent, cuts, -0.22, 0.18)
    return jnp.clip(values, -limit, limit).astype(kind)


def setup_inputs(seed: int = 0) -> dict:
    seeds = jax.random.split(jax.random.key(seed), 11)
    tokens = draw_tokens(jax.random.fold_in(seeds[10], 71), 0)
    cotangent = scatter_about(seeds[1], (TOKENS, D), 1.0, 6.0, ((0, 128),))
    w_query = scatter_about(seeds[2], (D, QUERY_FEATURES), D ** -0.5, 0.046875, ((0, 32),))
    w_key = scatter_about(seeds[3], (D, HEAD_SIZE), D ** -0.5, 0.046875, ((0, 32),))
    w_value = scatter_about(seeds[4], (D, HEAD_SIZE), D ** -0.5, 0.046875, ((0, 32),))
    w_output = scatter_about(seeds[5], (QUERY_FEATURES, D), QUERY_FEATURES ** -0.5, 0.375, ((1, 32),))
    adapter_down = scatter_about(seeds[6], (D, TENANTS, 2, R), D ** -0.5, 0.046875, ((0, 32), (1, 4)))
    adapter_up = scatter_about(seeds[7], (TENANTS, R, UPW), R ** -0.5, 1.5, ((0, 4),))
    tenant_slot = with_ends(jax.random.randint(seeds[8], (SAMPLES,), 0, TEN_DEV), jax.random.fold_in(seeds[8], 1), 0, TEN_DEV - 1).astype(jnp.int32)
    lengths = draw_lengths(jax.random.fold_in(seeds[10], 71), 0)
    return dict(tokens=tokens, cotangent=cotangent, w_query=w_query, w_key=w_key, w_value=w_value, w_output=w_output, adapter_down=adapter_down, adapter_up=adapter_up, tenant_slot=tenant_slot, lengths=lengths)


ADAPTER_SCALE = 2.0

def reference(tokens, cotangent, w_query, w_key, w_value, w_output, adapter_down, adapter_up, tenant_slot, lengths):
    frozen = jnp.concatenate([w_query, w_key, w_value], axis=1)
    inv_root = 1.0 / jnp.sqrt(jnp.float32(HEAD_SIZE))
    positions = jnp.arange(SEQ, dtype=jnp.int32)
    causal = positions[None, :] <= positions[:, None]
    groups = jnp.arange(SAMPLES, dtype=jnp.int32) % N_TENANT
    tok_all = tokens.reshape(SAMPLES, SEQ, D)
    cot_all = cotangent.reshape(SAMPLES, SEQ, D)

    def one_sample(carry, inputs):
        grad_down, grad_up = carry
        rows, cot, slot, length, group = inputs
        tenant = (TEN_DEV * group + slot).astype(jnp.int32)
        down_sel = lax.dynamic_index_in_dim(adapter_down, tenant, 1, keepdims=False)
        up_sel = lax.dynamic_index_in_dim(adapter_up, tenant, 0, keepdims=False)
        query_up_weight = up_sel[:, :QUERY_FEATURES]
        value_up_weight = up_sel[:, QUERY_FEATURES:]
        low_rank_rows = jnp.dot(rows, down_sel.reshape(D, 2 * R), preferred_element_type=jnp.float32)
        low_rank_rows = low_rank_rows.astype(jnp.bfloat16).reshape(SEQ, 2, R)
        frozen_output = jnp.dot(rows, frozen, preferred_element_type=jnp.float32)
        query_rows = (frozen_output[:, :QUERY_FEATURES] + ADAPTER_SCALE * jnp.dot(low_rank_rows[:, 0], query_up_weight, preferred_element_type=jnp.float32)).astype(jnp.bfloat16)
        key = frozen_output[:, QUERY_FEATURES:QUERY_FEATURES + HEAD_SIZE].astype(jnp.bfloat16)
        value_rows = (frozen_output[:, QUERY_FEATURES + HEAD_SIZE:] + ADAPTER_SCALE * jnp.dot(low_rank_rows[:, 1], value_up_weight, preferred_element_type=jnp.float32)).astype(jnp.bfloat16)
        valid = positions < length
        mask = causal & valid[None, :]
        keep = valid.astype(jnp.float32)[:, None]
        probs_list = []
        ctx_list = []
        for head_idx in range(QH):
            q_head = query_rows[:, head_idx * HEAD_SIZE:(head_idx + 1) * HEAD_SIZE]
            scores = jnp.dot(q_head, key.T, preferred_element_type=jnp.float32) * inv_root
            scores = jnp.where(mask, scores, jnp.float32(-1e+30))
            top = lax.optimization_barrier(jnp.max(scores, axis=1, keepdims=True))
            expo = jnp.where(mask, jnp.exp(scores - top), jnp.float32(0.0))
            probs = expo / lax.optimization_barrier(jnp.sum(expo, axis=1, keepdims=True))
            probs_list.append(probs)
            ctx_list.append(jnp.dot(probs.astype(jnp.bfloat16), value_rows, preferred_element_type=jnp.float32))
        context = (jnp.concatenate(ctx_list, axis=1) * keep).astype(jnp.bfloat16)
        output = jnp.dot(context, w_output, preferred_element_type=jnp.float32).astype(jnp.bfloat16)
        d_context = (jnp.dot(cot, w_output.T, preferred_element_type=jnp.float32) * keep).astype(jnp.bfloat16)
        value_acc = jnp.zeros((SEQ, HEAD_SIZE), jnp.float32)
        dq_list = []
        for head_idx in range(QH):
            probs = probs_list[head_idx]
            probs_b = probs.astype(jnp.bfloat16)
            d_ctx_head = d_context[:, head_idx * HEAD_SIZE:(head_idx + 1) * HEAD_SIZE]
            d_probs = jnp.dot(d_ctx_head, value_rows.T, preferred_element_type=jnp.float32)
            value_acc = value_acc + jnp.dot(probs_b.T, d_ctx_head, preferred_element_type=jnp.float32)
            delta = lax.optimization_barrier(jnp.sum(probs * d_probs, axis=1, keepdims=True))
            d_scores = (probs * (d_probs - delta)).astype(jnp.bfloat16)
            dq_list.append(jnp.dot(d_scores, key, preferred_element_type=jnp.float32) * inv_root)
        value_gradient = value_acc.astype(jnp.bfloat16)
        query_gradient = jnp.concatenate(dq_list, axis=1).astype(jnp.bfloat16)
        query_summand = jnp.dot(low_rank_rows[:, 0].T, query_gradient, preferred_element_type=jnp.float32)
        value_summand = jnp.dot(low_rank_rows[:, 1].T, value_gradient, preferred_element_type=jnp.float32)
        up_summand = ADAPTER_SCALE * jnp.concatenate([query_summand, value_summand], axis=1)
        query_middle = ADAPTER_SCALE * jnp.dot(query_gradient, query_up_weight.T, preferred_element_type=jnp.float32)
        value_middle = ADAPTER_SCALE * jnp.dot(value_gradient, value_up_weight.T, preferred_element_type=jnp.float32)
        mid = jnp.stack([query_middle, value_middle], axis=1).astype(jnp.bfloat16)
        term_down = jnp.dot(rows.T, mid.reshape(SEQ, 2 * R), preferred_element_type=jnp.float32).reshape(D, 2, R)
        grad_down = grad_down.at[:, tenant].add(term_down)
        grad_up = grad_up.at[tenant].add(up_summand)
        return ((grad_down, grad_up), output)
    start = (jnp.zeros((D, TENANTS, 2, R), jnp.float32), jnp.zeros((TENANTS, R, UPW), jnp.float32))
    (grad_down, grad_up), outputs = lax.scan(one_sample, start, (tok_all, cot_all, tenant_slot, lengths, groups))
    return (outputs.reshape(TOKENS, D), grad_down, grad_up)
```

```python
import jax
import jax.numpy as jnp
from jax import lax
from jax.experimental import pallas as pl
from jax.experimental.pallas import tpu as pltpu
from jax.sharding import PartitionSpec as P

ADAPTER_SCALE = 2.0
VMEM = 48 * 1024 * 1024
NT = (((1,), (1,)), ((), ()))
TN = (((0,), (0,)), ((), ()))
F32 = jnp.float32
BF16 = jnp.bfloat16


def dot(a, b, dims=(((1,), (0,)), ((), ()))):
    return lax.dot_general(a, b, dims, preferred_element_type=F32)


def params(**kw):
    return pltpu.CompilerParams(vmem_limit_bytes=VMEM, **kw)


def project_kernel(where, tok, cot, frozen, down_a, down_b, qkv, low, dctx):
    @pl.when(pl.program_id(0) == 0)
    def _():
        qkv[...] = jnp.zeros_like(qkv)
        low[...] = jnp.zeros_like(low)
        dctx[...] = jnp.zeros_like(dctx)

    q_cols = qkv.shape[1]
    qkv[...] += dot(tok[...], frozen[:, :q_cols])
    dctx[...] += dot(cot[...], frozen[:, q_cols:])
    shards, half = down_a.shape[0], down_a.shape[3]
    for i in range(shards):
        for h, down in enumerate((down_a, down_b)):
            at = (2 * i + h) * half
            low[...] += dot(tok[:, at : at + half], down[i, 0], NT)


def project(tokens, cotangent, gathered, tenant, slot, q_cols, d_cols, tenants):
    seq, width = tokens.shape
    block = 1024
    shard = width // (gathered.shape[0] // 128 // tenants)
    frozen_cols = q_cols + d_cols
    four = gathered.reshape(width // shard, tenants, shard // tenants, gathered.shape[1])
    per = block // shard
    pack = gathered.shape[1] - frozen_cols
    rows = 32
    grid_spec = pltpu.PrefetchScalarGridSpec(
        num_scalar_prefetch=1,
        grid=(width // block,),
        in_specs=[
            pl.BlockSpec((seq, block), lambda k, w: (0, k)),
            pl.BlockSpec((seq, block), lambda k, w: (0, k)),
            pl.BlockSpec((block, frozen_cols), lambda k, w: (k, 0)),
            pl.BlockSpec((per, 1, rows, pack), lambda k, w: (k, w[0], w[1], frozen_cols // pack)),
            pl.BlockSpec((per, 1, rows, pack), lambda k, w: (k, w[0], 2 + w[1], frozen_cols // pack)),
        ],
        out_specs=[
            pl.BlockSpec((seq, q_cols), lambda k, w: (0, 0)),
            pl.BlockSpec((seq, rows), lambda k, w: (0, 0)),
            pl.BlockSpec((seq, d_cols), lambda k, w: (0, 0)),
        ],
    )
    return pl.pallas_call(
        project_kernel,
        grid_spec=grid_spec,
        out_shape=[
            jax.ShapeDtypeStruct((seq, q_cols), F32),
            jax.ShapeDtypeStruct((seq, rows), F32),
            jax.ShapeDtypeStruct((seq, d_cols), F32),
        ],
        compiler_params=params(),
        name="project",
    )(jnp.stack([tenant, slot]), tokens, cotangent, gathered, four, four)


def attend_kernel(head, scalars, qkv, low_in, dctx_in, up, context, mid, up_sum):
    seq, total = qkv.shape
    heads = total // head - 2
    q_cols = heads * head
    length = scalars[1]
    inv_root = 1.0 / jnp.sqrt(F32(head))
    low = low_in[...].astype(BF16)
    added = ADAPTER_SCALE * dot(low, up[...])
    query = (qkv[:, :q_cols] + added[:, :q_cols]).astype(BF16)
    key = qkv[:, q_cols : q_cols + head].astype(BF16)
    value = (qkv[:, q_cols + head :] + added[:, q_cols:]).astype(BF16)
    row = lax.broadcasted_iota(jnp.int32, (seq, seq), 0)
    col = lax.broadcasted_iota(jnp.int32, (seq, seq), 1)
    mask = (col <= row) & (col < length)
    keep = lax.broadcasted_iota(jnp.int32, (seq, q_cols), 0) < length
    dctx = jnp.where(keep, dctx_in[...], 0.0).astype(BF16)
    d_value = jnp.zeros((seq, head), F32)
    outs, dqs = [], []
    for h in range(heads):
        cols = slice(h * head, (h + 1) * head)
        scores = dot(query[:, cols], key, NT) * inv_root
        scores = jnp.where(mask, scores, F32(-1e30))
        top = jnp.max(scores, axis=1, keepdims=True)
        expo = jnp.where(mask, jnp.exp(scores - top), 0.0)
        probs = expo / jnp.sum(expo, axis=1, keepdims=True)
        probs_b = probs.astype(BF16)
        outs.append(dot(probs_b, value))
        d_head = dctx[:, cols]
        d_probs = dot(d_head, value, NT)
        d_value += dot(probs_b, d_head, TN)
        delta = jnp.sum(probs * d_probs, axis=1, keepdims=True)
        d_scores = (probs * (d_probs - delta)).astype(BF16)
        dqs.append(dot(d_scores, key) * inv_root)
    context[...] = jnp.where(keep, jnp.concatenate(outs, axis=1), 0.0).astype(BF16)
    d_all = jnp.concatenate(dqs + [d_value], axis=1).astype(BF16)
    mid[...] = (ADAPTER_SCALE * dot(up[...], d_all, NT)).astype(BF16)
    sums = ADAPTER_SCALE * dot(low, d_all, TN)
    rank = sums.shape[0] // 2
    slot = jnp.full((rank, head), scalars[0], jnp.int32).astype(F32)
    up_sum[...] = jnp.concatenate([sums[:rank, :q_cols], sums[rank:, q_cols:], slot], axis=1).astype(BF16)


def attend(scalars, qkv, low, dctx, up, head):
    seq, q_cols = dctx.shape
    vmem = pl.BlockSpec(memory_space=pltpu.VMEM)
    rank2 = low.shape[1]
    return pl.pallas_call(
        lambda *refs: attend_kernel(head, *refs),
        in_specs=[pl.BlockSpec(memory_space=pltpu.SMEM)] + [vmem] * 4,
        out_specs=[vmem] * 3,
        out_shape=[
            jax.ShapeDtypeStruct((seq, q_cols), BF16),
            jax.ShapeDtypeStruct((rank2, seq), BF16),
            jax.ShapeDtypeStruct((rank2 // 2, q_cols + 2 * head), BF16),
        ],
        compiler_params=params(),
        name="attend",
    )(scalars, qkv, low, dctx, up)


def term_kernel(mid, up_sum, tok, out):
    rows = mid.shape[0]
    for i in range(out.shape[0]):
        width = out.shape[2]
        out[i, :rows, :] = dot(mid[...], tok[:, i * width : (i + 1) * width]).astype(BF16)
        out[i, rows:, :] = up_sum[...]


def term(mid, up_sum, tokens, parts):
    seq, width = tokens.shape
    per = 4
    shard = width // parts
    rows = mid.shape[0] + up_sum.shape[0]
    return pl.pallas_call(
        term_kernel,
        grid=(parts // per,),
        in_specs=[
            pl.BlockSpec(mid.shape, lambda k: (0, 0)),
            pl.BlockSpec(up_sum.shape, lambda k: (0, 0)),
            pl.BlockSpec((seq, per * shard), lambda k: (0, k)),
        ],
        out_specs=pl.BlockSpec((per, rows, shard), lambda k: (k, 0, 0)),
        out_shape=jax.ShapeDtypeStruct((parts, rows, shard), BF16),
        compiler_params=params(),
        name="term",
    )(mid, up_sum, tokens)


def output_kernel(context, w, out):
    out[...] = dot(context[...], w[...], NT).astype(BF16)


def output_of(context, gathered, first, cost):
    seq, cols = context.shape
    width = gathered.shape[0]
    block = 1024
    return pl.pallas_call(
        output_kernel,
        grid=(width // block,),
        in_specs=[
            pl.BlockSpec((seq, cols), lambda k: (0, 0)),
            pl.BlockSpec((block, cols), lambda k: (k, first // cols)),
        ],
        out_specs=pl.BlockSpec((seq, block), lambda k: (0, k)),
        out_shape=jax.ShapeDtypeStruct((seq, width), BF16),
        compiler_params=params(),
        cost_estimate=cost,
        name="output",
    )(context, gathered)


def total_kernel(got, down, up):
    rows = down.shape[1]
    cols = up.shape[2]
    sums = [jnp.zeros(got.shape[1:], F32) for _ in range(2)]
    for f in range(got.shape[0]):
        part = got[f].astype(F32)
        one = part[rows : rows + 1, cols : cols + 1]
        sums[0] += part * (1.0 - one)
        sums[1] += part * one
    for s in range(2):
        down[s] = sums[s][:rows]
        up[s] = sums[s][rows:, :cols]


def total(got, rows, cols):
    parts, every, shard = got.shape
    vmem = pl.BlockSpec(memory_space=pltpu.VMEM)
    return pl.pallas_call(
        total_kernel,
        in_specs=[vmem],
        out_specs=[vmem] * 2,
        out_shape=[
            jax.ShapeDtypeStruct((2, rows, shard), F32),
            jax.ShapeDtypeStruct((2, every - rows, cols), F32),
        ],
        compiler_params=params(),
        name="total",
    )(got)


def body(
    tokens,
    cotangent,
    w_query,
    w_key,
    w_value,
    w_output,
    adapter_down,
    adapter_up,
    tenant_slot,
    lengths,
):
    seq, width = tokens.shape
    q_cols = w_query.shape[1]
    head = w_key.shape[1]
    shard, slots, _, rank = adapter_down.shape
    tenants = lax.axis_size("tenant")
    parts = lax.axis_size("fsdp")
    tenant = lax.axis_index("tenant").astype(jnp.int32)
    slot = tenant_slot[0]
    quarter = shard // tenants

    def mine(w):
        return lax.dynamic_slice_in_dim(w, tenant * quarter, quarter, 0)

    down = adapter_down.reshape(shard, slots * 2 * rank).T
    down = jnp.concatenate([down[:, : shard // 2], down[:, shard // 2 :]], axis=0)
    local = jnp.concatenate(
        [mine(w_query), mine(w_key), mine(w_value), mine(w_output.T), down], axis=1
    )
    gathered = lax.all_gather(local, ("fsdp", "tenant"), axis=0, tiled=True)
    up = lax.dynamic_index_in_dim(adapter_up, slot, 0, keepdims=False)
    at_query = jnp.arange(q_cols + head)[None, :] < q_cols
    up = jnp.concatenate(
        [jnp.where(at_query, up, 0), jnp.where(at_query, 0, up)], axis=0
    ).astype(BF16)
    qkv_cols = q_cols + 2 * head
    qkv, low, dctx = project(
        tokens, cotangent, gathered, tenant, slot, qkv_cols, q_cols, tenants
    )
    scalars = jnp.stack([slot, lengths[0]])
    context, mid, up_sum = attend(scalars, qkv, low, dctx, up, head)
    sent = term(mid, up_sum, tokens, parts)
    got = lax.all_to_all(sent, "fsdp", split_axis=0, concat_axis=0, tiled=True)
    cost = pl.CostEstimate(
        flops=2 * seq * q_cols * width, bytes_accessed=4 * seq * width, transcendentals=0
    )
    output = output_of(context, gathered, qkv_cols, cost)
    down_sum, grad_up = total(got, 2 * rank, q_cols + head)
    grad_down = down_sum.reshape(slots * 2 * rank, shard).T.reshape(shard, slots, 2, rank)
    return (output, grad_down, grad_up)


def solution(mesh):
    placed = (
        P(("fsdp", "tenant"), None),
        P(("fsdp", "tenant"), None),
        P("fsdp", None),
        P("fsdp", None),
        P("fsdp", None),
        P(None, "fsdp"),
        P("fsdp", "tenant", None, None),
        P("tenant", None, None),
        P(("fsdp", "tenant")),
        P(("fsdp", "tenant")),
    )
    return jax.shard_map(
        body,
        mesh=mesh,
        in_specs=placed,
        out_specs=(
            P(("fsdp", "tenant"), None),
            P("fsdp", "tenant", None, None),
            P("tenant", None, None),
        ),
        check_vma=False,
    )
```

```python
import functools

import jax
import jax.numpy as jnp
from jax import lax
from jax.experimental import pallas as pl
from jax.experimental.pallas import tpu as pltpu
from jax.sharding import PartitionSpec as P

ADAPTER_SCALE = 2.0
Y, Z = 4, 4
VMEM = 48 * 1024 * 1024
NT = (((1,), (1,)), ((), ()))
TN = (((0,), (0,)), ((), ()))
F32 = jnp.float32
BF16 = jnp.bfloat16


def dot(a, b, dims=(((1,), (0,)), ((), ()))):
    return lax.dot_general(a, b, dims, preferred_element_type=F32)


def params(**kw):
    return pltpu.CompilerParams(vmem_limit_bytes=VMEM, **kw)


def pack_kernel(where, w_query, w_key, w_value, down, w_output, out):
    head, low = w_key.shape[1], down.shape[0]
    half = out.shape[1]
    out[:half, :] = w_query[...]
    out[half : 2 * half, :head] = w_key[...]
    out[half : 2 * half, head:] = w_value[...]
    for h in range(2):
        out[2 * half + h * low : 2 * half + (h + 1) * low, :] = down[:, h * half : (h + 1) * half]
    out[2 * half + 2 * low :, :] = w_output[...]


def pack(where, w_query, w_key, w_value, down, w_output):
    half = w_query.shape[0] // 2
    q_cols, head, low = w_query.shape[1], w_key.shape[1], down.shape[0]
    rows = lambda cols: pl.BlockSpec((half, cols), lambda k, w: (w[0], 0))
    return pl.pallas_call(
        pack_kernel,
        grid_spec=pltpu.PrefetchScalarGridSpec(
            num_scalar_prefetch=1,
            grid=(1,),
            in_specs=[
                rows(q_cols),
                rows(head),
                rows(head),
                pl.BlockSpec(down.shape, lambda k, w: (0, 0)),
                pl.BlockSpec((q_cols, half), lambda k, w: (0, w[0])),
            ],
            out_specs=pl.BlockSpec((3 * half + 2 * low, half), lambda k, w: (0, 0)),
        ),
        out_shape=jax.ShapeDtypeStruct((3 * half + 2 * low, half), BF16),
        compiler_params=params(),
        name="pack",
    )(where, w_query, w_key, w_value, down, w_output)


def pick_kernel(where, a, b, out_a, out_b):
    piece = 256
    for side in range(2):

        @pl.when(where[0] == side)
        def _():
            for full, out in ((a, out_a), (b, out_b)):
                for i in range(out.shape[1] // piece):
                    at = (2 * i + 1 - side) * piece
                    out[:, i * piece : (i + 1) * piece] = full[:, at : at + piece]


def pick(a, b, where):
    seq, width = a.shape
    block = 4096
    return pl.pallas_call(
        pick_kernel,
        grid_spec=pltpu.PrefetchScalarGridSpec(
            num_scalar_prefetch=1,
            grid=(width // block,),
            in_specs=[pl.BlockSpec((seq, block), lambda k, w: (0, k))] * 2,
            out_specs=[pl.BlockSpec((seq, block // 2), lambda k, w: (0, k))] * 2,
        ),
        out_shape=[jax.ShapeDtypeStruct((seq, width // 2), BF16)] * 2,
        compiler_params=params(),
        cost_estimate=pl.CostEstimate(flops=0, bytes_accessed=6 * seq * width, transcendentals=0),
        name="pick",
    )(where, a, b)


def arrive_kernel(where, tok, cot_a, cot_b, mate_tok, mate_cot, near, far, *refs, fresh):
    *after, kept = refs[-4:]
    step = pl.program_id(0)

    @pl.when(step == 0)
    def _():
        for i, new in enumerate(after):
            new[...] = jnp.zeros_like(new) if fresh else refs[i][...]

    mine, other, low = after
    core, slot, x_hi = where[0], where[1], where[2]
    half = near.shape[3]
    first = near.shape[2] - half

    def add(pair):
        own = jnp.concatenate(
            [tok[:, pl.ds(pl.multiple_of((2 * x + core) * half, half), half)] for x in range(2)], axis=1
        )
        at = [x ^ x_hi for x in range(2)]
        for g in range(2):
            cols = slice(g * half, (g + 1) * half)
            w = jnp.concatenate([pair[0, i, cols, :] for i in at], axis=0)
            mine[:, cols] += dot(own, w)
            other[:, cols] += dot(mate_tok[...], w)
        w = [pair[0, i, first:, :] for i in at]
        cols = slice(2 * half, 3 * half)
        both = jnp.concatenate(w, axis=1)
        mine[:, cols] += dot(jnp.concatenate([cot_a[...], cot_b[...]], axis=1), both, NT)
        other[:, cols] += dot(mate_cot[...], both, NT)
        for x in range(2):
            kept[0, x] = w[x]
        down = [
            pair[0, i, pl.ds(pl.multiple_of(2 * half + h * 64 + slot * 32, 32), 32), :]
            for i in at
            for h in range(2)
        ]
        low[...] += dot(tok[...], jnp.concatenate(down, axis=1), NT)

    count = pl.num_programs(0) // 2

    @pl.when(step < count)
    def _():
        add(near)

    @pl.when(step >= count)
    def _():
        add(far)


def arrive(where, tokens, cotangent, mate_tok, mate_cot, first, second, sums, out_shape):
    seq = tokens.shape[0]
    count, _, rows, half = first[0].shape
    steps = first[1] + second[1]

    def at(k, w):
        early = jnp.int32(steps[0])
        for i in range(1, len(steps)):
            early = jnp.where(k == i, steps[i], early)
        late = jnp.where(k < count, first[2], second[2])
        y = (w[3] - jnp.where(w[0] == 0, late, early) + Y) % Y
        z = (w[4] - jnp.where(w[0] == 0, early, late) + Z) % Z
        return y * Z + z

    whole = [pl.BlockSpec(x.shape, lambda k, w: (0, 0)) for x in out_shape[:3]]
    block = (1, 2, rows, half)
    fresh = not sums
    return pl.pallas_call(
        functools.partial(arrive_kernel, fresh=fresh),
        grid_spec=pltpu.PrefetchScalarGridSpec(
            num_scalar_prefetch=1,
            grid=(2 * count,),
            in_specs=[
                pl.BlockSpec((seq, 4 * half), lambda k, w: (0, at(k, w))),
                pl.BlockSpec((seq, half), lambda k, w: (0, 4 * at(k, w) + w[0])),
                pl.BlockSpec((seq, half), lambda k, w: (0, 4 * at(k, w) + 2 + w[0])),
                pl.BlockSpec((seq, 2 * half), lambda k, w: (0, at(k, w))),
                pl.BlockSpec((seq, 2 * half), lambda k, w: (0, at(k, w))),
                pl.BlockSpec(block, lambda k, w: (jnp.minimum(k, count - 1), 0, 0, 0)),
                pl.BlockSpec(block, lambda k, w: (jnp.maximum(k - count, 0), 0, 0, 0)),
            ]
            + ([] if fresh else whole + [pl.BlockSpec(memory_space=pl.ANY)]),
            out_specs=whole + [pl.BlockSpec((1, 2, half, half), lambda k, w: (at(k, w), 0, 0, 0))],
        ),
        out_shape=out_shape,
        input_output_aliases={} if fresh else {11: 3},
        compiler_params=params(),
        cost_estimate=pl.CostEstimate(flops=count * 2**30, bytes_accessed=count * 2**22, transcendentals=0),
        name="arrive",
    )(where, tokens, cotangent, cotangent, mate_tok, mate_cot, first[0], second[0], *sums)


def attend_kernel(head, scalars, mine, other, low_in, up, context, mid, up_sum):
    seq, total = mine.shape
    q_cols = (total - 2 * head) // 2
    heads = q_cols // head
    length = scalars[1]
    inv_root = 1.0 / jnp.sqrt(F32(head))
    low = low_in[...].astype(BF16)
    added = ADAPTER_SCALE * dot(low, up[...])
    summed = mine[...] + other[...]
    qkv, dctx = summed[:, : total - q_cols], summed[:, total - q_cols :]
    query = (qkv[:, :q_cols] + added[:, :q_cols]).astype(BF16)
    key = qkv[:, q_cols : q_cols + head].astype(BF16)
    value = (qkv[:, q_cols + head :] + added[:, q_cols:]).astype(BF16)
    row = lax.broadcasted_iota(jnp.int32, (seq, seq), 0)
    col = lax.broadcasted_iota(jnp.int32, (seq, seq), 1)
    mask = (col <= row) & (col < length)
    keep = lax.broadcasted_iota(jnp.int32, (seq, q_cols), 0) < length
    dctx = jnp.where(keep, dctx, 0.0).astype(BF16)
    d_value = jnp.zeros((seq, head), F32)
    outs, dqs = [], []
    for h in range(heads):
        cols = slice(h * head, (h + 1) * head)
        scores = dot(query[:, cols], key, NT) * inv_root
        scores = jnp.where(mask, scores, F32(-1e30))
        top = jnp.max(scores, axis=1, keepdims=True)
        expo = jnp.where(mask, jnp.exp(scores - top), 0.0)
        probs = expo / jnp.sum(expo, axis=1, keepdims=True)
        probs_b = probs.astype(BF16)
        outs.append(dot(probs_b, value))
        d_head = dctx[:, cols]
        d_probs = dot(d_head, value, NT)
        d_value += dot(probs_b, d_head, TN)
        delta = jnp.sum(probs * d_probs, axis=1, keepdims=True)
        d_scores = (probs * (d_probs - delta)).astype(BF16)
        dqs.append(dot(d_scores, key) * inv_root)
    context[...] = jnp.where(keep, jnp.concatenate(outs, axis=1), 0.0).astype(BF16)
    d_all = jnp.concatenate(dqs + [d_value], axis=1).astype(BF16)
    mid[...] = (ADAPTER_SCALE * dot(up[...], d_all, NT)).astype(BF16)
    sums = ADAPTER_SCALE * dot(low, d_all, TN)
    rank = sums.shape[0] // 2
    slot = jnp.full((rank, head), scalars[0], jnp.int32).astype(F32)
    up_sum[...] = jnp.concatenate([sums[:rank, :q_cols], sums[rank:, q_cols:], slot], axis=1).astype(BF16)


def attend(scalars, mine, other, low, up, head):
    seq, total = mine.shape
    q_cols = (total - 2 * head) // 2
    vmem = pl.BlockSpec(memory_space=pltpu.VMEM)
    rank2 = low.shape[1]
    return pl.pallas_call(
        lambda *refs: attend_kernel(head, *refs),
        in_specs=[pl.BlockSpec(memory_space=pltpu.SMEM)] + [vmem] * 4,
        out_specs=[vmem] * 3,
        out_shape=[
            jax.ShapeDtypeStruct((seq, q_cols), BF16),
            jax.ShapeDtypeStruct((rank2, seq), BF16),
            jax.ShapeDtypeStruct((rank2 // 2, q_cols + 2 * head), BF16),
        ],
        compiler_params=params(),
        name="attend",
    )(scalars, mine, other, low, up)


def term_kernel(mid, up_sum, tok, out):
    rows = mid.shape[0]
    for i in range(out.shape[0]):
        width = out.shape[2]
        out[i, :rows, :] = dot(mid[...], tok[:, i * width : (i + 1) * width]).astype(BF16)
        out[i, rows:, :] = up_sum[...]


def term(mid, up_sum, tokens, parts):
    seq, width = tokens.shape
    per = 8
    shard = width // parts
    rows = mid.shape[0] + up_sum.shape[0]
    return pl.pallas_call(
        term_kernel,
        grid=(parts // per,),
        in_specs=[
            pl.BlockSpec(mid.shape, lambda k: (0, 0)),
            pl.BlockSpec(up_sum.shape, lambda k: (0, 0)),
            pl.BlockSpec((seq, per * shard), lambda k: (0, k)),
        ],
        out_specs=pl.BlockSpec((per, rows, shard), lambda k: (k, 0, 0)),
        out_shape=jax.ShapeDtypeStruct((parts, rows, shard), BF16),
        compiler_params=params(),
        name="term",
    )(mid, up_sum, tokens)


def output_kernel(where, context, own, theirs, out):
    pairs, _, rows, half = own.shape
    for core in range(2):

        @pl.when(where[0] == core)
        def _():
            halves = (own, theirs) if core == 0 else (theirs, own)
            for p in range(pairs):
                for x in range(2):
                    w = jnp.concatenate([h[p, x] for h in halves], axis=1)
                    at = (2 * p + x) * 2 * half
                    out[:, at : at + 2 * half] = dot(context[...], w).astype(BF16)


def output_of(where, context, own, theirs, cost):
    seq, cols = context.shape
    count, _, rows, half = own.shape
    per = 2
    weights = pl.BlockSpec((per, 2, rows, half), lambda k, w: (k, 0, 0, 0))
    return pl.pallas_call(
        output_kernel,
        grid_spec=pltpu.PrefetchScalarGridSpec(
            num_scalar_prefetch=1,
            grid=(count // per,),
            in_specs=[pl.BlockSpec((seq, cols), lambda k, w: (0, 0)), weights, weights],
            out_specs=pl.BlockSpec((seq, per * 4 * half), lambda k, w: (0, k)),
        ),
        out_shape=jax.ShapeDtypeStruct((seq, count * 4 * half), BF16),
        compiler_params=params(),
        cost_estimate=cost,
        name="output",
    )(where, context, own, theirs)


def total_kernel(got, down, up):
    rows = down.shape[1]
    cols = up.shape[2]
    sums = [jnp.zeros(got.shape[1:], F32) for _ in range(2)]
    for f in range(got.shape[0]):
        part = got[f].astype(F32)
        one = part[rows : rows + 1, cols : cols + 1]
        sums[0] += part * (1.0 - one)
        sums[1] += part * one
    for s in range(2):
        down[s] = sums[s][:rows]
        up[s] = sums[s][rows:, :cols]


def total(got, rows, cols):
    parts, every, shard = got.shape
    vmem = pl.BlockSpec(memory_space=pltpu.VMEM)
    return pl.pallas_call(
        total_kernel,
        in_specs=[vmem],
        out_specs=[vmem] * 2,
        out_shape=[
            jax.ShapeDtypeStruct((2, rows, shard), F32),
            jax.ShapeDtypeStruct((2, every - rows, cols), F32),
        ],
        compiler_params=params(),
        name="total",
    )(got)


def body(
    tokens,
    cotangent,
    w_query,
    w_key,
    w_value,
    w_output,
    adapter_down,
    adapter_up,
    tenant_slot,
    lengths,
):
    seq, width = tokens.shape
    q_cols = w_query.shape[1]
    head = w_key.shape[1]
    shard, slots, _, rank = adapter_down.shape
    tenants = lax.axis_size("tenant")
    parts = lax.axis_size("fsdp")
    tenant = lax.axis_index("tenant").astype(jnp.int32)
    slot = tenant_slot[0]

    place = lax.axis_index("fsdp").astype(jnp.int32)
    y, z, x_hi = place // (2 * Z), place // 2 % Z, place % 2
    core = tenant % 2

    def shift(array, hops, late):
        to = []
        for f in range(parts):
            for t in range(tenants):
                along_y = (t % 2 == 0) == late
                f_y = (f // (2 * Z) + hops * along_y) % Y
                f_z = (f // 2 + hops * (not along_y)) % Z
                to.append((f * tenants + t, ((f_y * Z + f_z) * 2 + f % 2) * tenants + t))
        return lax.ppermute(array, ("fsdp", "tenant"), to)

    def swap(array):
        return lax.ppermute(array, "tenant", [(t, t ^ 1) for t in range(tenants)])

    where = jnp.stack([core, slot, x_hi, y, z])
    down = adapter_down.reshape(shard, slots * 2 * rank).T
    piece = pack(where, w_query, w_key, w_value, down, w_output)
    flipped = lax.ppermute(piece, "fsdp", [(f, f ^ 1) for f in range(parts)])
    hops = (1, 3, 2)
    early = {j: shift(piece, j, False) for j in hops}
    halves = pick(tokens, cotangent, where)
    flipped, early, halves = lax.optimization_barrier((flipped, early, halves))
    early_flipped = {j: shift(flipped, j, False) for j in hops}
    mate_tok, mate_cot = (swap(half) for half in halves)
    early[0], early_flipped[0] = piece, flipped

    def group(steps):
        return jnp.stack([jnp.stack([early[j], early_flipped[j]]) for j in steps])

    near, far = (0, 1), (3, 2)
    here_near, here_far = group(near), group(far)
    ahead_near, behind_far = shift(here_near, 1, True), shift(here_far, -1, True)
    ahead_far, behind_near = shift(here_far, 1, True), shift(here_near, -1, True)
    out_shape = [jax.ShapeDtypeStruct((seq, 2 * (q_cols + head)), F32)] * 2 + [
        jax.ShapeDtypeStruct((seq, 2 * rank), F32),
        jax.ShapeDtypeStruct((parts // 2, 2, q_cols, shard // 2), BF16),
    ]

    def add(first, second, sums):
        return arrive(where, tokens, cotangent, mate_tok, mate_cot, first, second, sums, out_shape)

    sums = add((here_near, near, 0), (here_far, far, 0), ())
    ahead_near, behind_far, sums = lax.optimization_barrier((ahead_near, behind_far, sums))
    far_ahead, far_behind = shift(ahead_near, 1, True), shift(behind_far, -1, True)
    sums = add((ahead_near, near, 1), (behind_far, far, 3), sums)
    sums = add((ahead_far, far, 1), (behind_near, near, 3), sums)
    sums = add((far_ahead, near, 2), (far_behind, far, 2), sums)
    summed, other, low, kept = sums
    other = swap(other)
    other, kept = lax.optimization_barrier((other, kept))
    theirs = swap(kept)

    up = lax.dynamic_index_in_dim(adapter_up, slot, 0, keepdims=False)
    at_query = jnp.arange(q_cols + head)[None, :] < q_cols
    up = jnp.concatenate(
        [jnp.where(at_query, up, 0), jnp.where(at_query, 0, up)], axis=0
    ).astype(BF16)
    scalars = jnp.stack([slot, lengths[0]])
    context, mid, up_sum = attend(scalars, summed, other, low, up, head)
    sent = term(mid, up_sum, tokens, parts)
    got = lax.all_to_all(sent, "fsdp", split_axis=0, concat_axis=0, tiled=True)
    cost = pl.CostEstimate(
        flops=2 * seq * q_cols * width, bytes_accessed=4 * seq * width, transcendentals=0
    )
    output = output_of(where, context, kept, theirs, cost)
    got, output = lax.optimization_barrier((got, output))
    down_sum, grad_up = total(got, 2 * rank, q_cols + head)
    grad_down = down_sum.reshape(slots * 2 * rank, shard).T.reshape(shard, slots, 2, rank)
    return (output, grad_down, grad_up)


def solution(mesh):
    placed = (
        P(("fsdp", "tenant"), None),
        P(("fsdp", "tenant"), None),
        P("fsdp", None),
        P("fsdp", None),
        P("fsdp", None),
        P(None, "fsdp"),
        P("fsdp", "tenant", None, None),
        P("tenant", None, None),
        P(("fsdp", "tenant")),
        P(("fsdp", "tenant")),
    )
    return jax.shard_map(
        body,
        mesh=mesh,
        in_specs=placed,
        out_specs=(
            P(("fsdp", "tenant"), None),
            P("fsdp", "tenant", None, None),
            P("tenant", None, None),
        ),
        check_vma=False,
    )
```

```python
import functools

import jax
import jax.numpy as jnp
from jax import lax
from jax.experimental import pallas as pl
from jax.experimental.pallas import tpu as pltpu
from jax.sharding import PartitionSpec as P

ADAPTER_SCALE = 2.0
Y, Z = 4, 4
VMEM = 48 * 1024 * 1024
NT = (((1,), (1,)), ((), ()))
TN = (((0,), (0,)), ((), ()))
F32 = jnp.float32
BF16 = jnp.bfloat16


def dot(a, b, dims=(((1,), (0,)), ((), ()))):
    return lax.dot_general(a, b, dims, preferred_element_type=F32)


def params(**kw):
    return pltpu.CompilerParams(vmem_limit_bytes=VMEM, **kw)


def pack_kernel(where, w_query, w_key, w_value, down, w_output, out):
    head, low = w_key.shape[1], down.shape[0]
    half = out.shape[1]
    out[:half, :] = w_query[...]
    out[half : 2 * half, :head] = w_key[...]
    out[half : 2 * half, head:] = w_value[...]
    for h in range(2):
        out[2 * half + h * low : 2 * half + (h + 1) * low, :] = down[:, h * half : (h + 1) * half]
    out[2 * half + 2 * low :, :] = w_output[...]


def pack(where, w_query, w_key, w_value, down, w_output):
    half = w_query.shape[0] // 2
    q_cols, head, low = w_query.shape[1], w_key.shape[1], down.shape[0]
    rows = lambda cols: pl.BlockSpec((half, cols), lambda k, w: (w[0], 0))
    return pl.pallas_call(
        pack_kernel,
        grid_spec=pltpu.PrefetchScalarGridSpec(
            num_scalar_prefetch=1,
            grid=(1,),
            in_specs=[
                rows(q_cols),
                rows(head),
                rows(head),
                pl.BlockSpec(down.shape, lambda k, w: (0, 0)),
                pl.BlockSpec((q_cols, half), lambda k, w: (0, w[0])),
            ],
            out_specs=pl.BlockSpec((3 * half + 2 * low, half), lambda k, w: (0, 0)),
        ),
        out_shape=jax.ShapeDtypeStruct((3 * half + 2 * low, half), BF16),
        compiler_params=pltpu.CompilerParams(vmem_limit_bytes=56 * 1024 * 1024),
        name="pack",
    )(where, w_query, w_key, w_value, down, w_output)


def arrive_kernel(where, *refs, pieces, fresh):
    tok, cot, mate_tok, mate_cot = refs[0:2], refs[2:4], refs[4:6], refs[6:8]
    arrived, refs = refs[8 : 8 + pieces], refs[8 + pieces :]
    both, low, kept = refs[-3:]
    step = pl.program_id(0)

    if fresh:

        @pl.when(step == 0)
        def _():
            for new in (both, low):
                new[...] = jnp.zeros_like(new)

    core, slot = where[0], where[1]
    half = arrived[0].shape[2]
    first = arrived[0].shape[1] - half

    def add(shard):
        side = pl.multiple_of(core * half, half)
        rows = jnp.concatenate(
            [
                jnp.concatenate([t[:, pl.ds(side, half)] for t in tok], axis=1),
                jnp.concatenate([t[...] for t in mate_tok], axis=1),
            ],
            axis=0,
        )
        for g in range(2):
            cols = slice(g * half, (g + 1) * half)
            both[:, cols] += dot(rows, jnp.concatenate([shard[i, cols, :] for i in range(2)], axis=0))
        rows = jnp.concatenate([jnp.concatenate([t[...] for t in two], axis=1) for two in (cot, mate_cot)], axis=0)
        w = jnp.concatenate([shard[i, first:, :] for i in range(2)], axis=1)
        both[:, 2 * half :] += dot(rows, w, NT)
        kept[...] = shard[:, first:, :]
        down = [
            shard[i, pl.ds(pl.multiple_of(2 * half + h * 64 + slot * 32, 32), 32), :]
            for i in range(2)
            for h in range(2)
        ]
        rows = jnp.concatenate([t[...] for t in tok], axis=1)
        low[...] += dot(rows, jnp.concatenate(down, axis=1), NT)

    for i in range(pieces):

        @pl.when(step == i)
        def _():
            add(arrived[i])


def place(w, early, late):
    y = (w[3] - jnp.where(w[0] == 0, late, early) + Y) % Y
    z = (w[4] - jnp.where(w[0] == 0, early, late) + Z) % Z
    return y * Z + z


def arrive(where, tokens, cotangent, mate_tok, mate_cot, pieces, lates, flip, base, sums, out_shape):
    seq = tokens.shape[0]
    rows, half = pieces[0][0].shape[1:]

    def at(k, w, p):
        late = jnp.where(k < 2, lates[0], lates[-1])
        return 2 * place(w, 2 * (k % 2) + p, late) + (w[2] ^ flip)

    def two(cols, index):
        return [pl.BlockSpec((seq, cols), lambda k, w, p=p: (0, index(k, w, p))) for p in range(2)]

    core_half = lambda k, w, p: 2 * at(k, w, p) + w[0]
    whole = [pl.BlockSpec(memory_space=pltpu.VMEM)] * 2
    fresh = [x is None for x in sums]
    given = [x for x in sums if x is not None]
    inputs = [tokens] * 2 + [cotangent] * 2 + [mate_tok] * 2 + [mate_cot] * 2 + [a for a, _ in pieces]
    kept_at = [i for i in range(3) if not fresh[i]]
    kept_spec = [] if fresh[2] else [pl.BlockSpec(memory_space=pl.ANY)]
    return pl.pallas_call(
        functools.partial(arrive_kernel, pieces=len(pieces), fresh=fresh[0]),
        grid_spec=pltpu.PrefetchScalarGridSpec(
            num_scalar_prefetch=1,
            grid=(len(pieces),),
            in_specs=two(2 * half, at)
            + two(half, core_half) * 3
            + [pl.BlockSpec((2, rows, half), lambda k, w, i=i: (i, 0, 0)) for _, i in pieces]
            + ([] if fresh[0] else whole)
            + kept_spec,
            out_specs=whole + [pl.BlockSpec((2, half, half), lambda k, w: (base + k, 0, 0))],
        ),
        out_shape=out_shape,
        input_output_aliases=dict(zip(range(1 + len(inputs), 1 + len(inputs) + len(given)), kept_at)),
        compiler_params=params(),
        cost_estimate=pl.CostEstimate(flops=len(pieces) * 2**29, bytes_accessed=len(pieces) * 2**21, transcendentals=0),
        name="arrive",
    )(where, *inputs, *given)


def attend_kernel(head, scalars, mine, other, low_in, up, context, mid, up_sum):
    seq, total = other.shape
    q_cols = (total - 2 * head) // 2
    heads = q_cols // head
    length = scalars[1]
    inv_root = 1.0 / jnp.sqrt(F32(head))
    low = low_in[...].astype(BF16)
    added = ADAPTER_SCALE * dot(low, up[...])
    summed = mine[:seq, :] + other[...]
    qkv, dctx = summed[:, : total - q_cols], summed[:, total - q_cols :]
    query = (qkv[:, :q_cols] + added[:, :q_cols]).astype(BF16)
    key = qkv[:, q_cols : q_cols + head].astype(BF16)
    value = (qkv[:, q_cols + head :] + added[:, q_cols:]).astype(BF16)
    row = lax.broadcasted_iota(jnp.int32, (seq, seq), 0)
    col = lax.broadcasted_iota(jnp.int32, (seq, seq), 1)
    mask = (col <= row) & (col < length)
    keep = lax.broadcasted_iota(jnp.int32, (seq, q_cols), 0) < length
    dctx = jnp.where(keep, dctx, 0.0).astype(BF16)
    d_value = jnp.zeros((seq, head), F32)
    outs, dqs = [], []
    for h in range(heads):
        cols = slice(h * head, (h + 1) * head)
        scores = dot(query[:, cols], key, NT) * inv_root
        scores = jnp.where(mask, scores, F32(-1e30))
        top = jnp.max(scores, axis=1, keepdims=True)
        expo = jnp.where(mask, jnp.exp(scores - top), 0.0)
        probs = expo / jnp.sum(expo, axis=1, keepdims=True)
        probs_b = probs.astype(BF16)
        outs.append(dot(probs_b, value))
        d_head = dctx[:, cols]
        d_probs = dot(d_head, value, NT)
        d_value += dot(probs_b, d_head, TN)
        delta = jnp.sum(probs * d_probs, axis=1, keepdims=True)
        d_scores = (probs * (d_probs - delta)).astype(BF16)
        dqs.append(dot(d_scores, key) * inv_root)
    context[...] = jnp.where(keep, jnp.concatenate(outs, axis=1), 0.0).astype(BF16)
    d_all = jnp.concatenate(dqs + [d_value], axis=1).astype(BF16)
    mid[...] = (ADAPTER_SCALE * dot(up[...], d_all, NT)).astype(BF16)
    sums = ADAPTER_SCALE * dot(low, d_all, TN)
    rank = sums.shape[0] // 2
    slot = jnp.full((rank, head), scalars[0], jnp.int32).astype(F32)
    up_sum[...] = jnp.concatenate([sums[:rank, :q_cols], sums[rank:, q_cols:], slot], axis=1).astype(BF16)


def attend(scalars, mine, other, low, up, head):
    seq, total = other.shape
    q_cols = (total - 2 * head) // 2
    vmem = pl.BlockSpec(memory_space=pltpu.VMEM)
    rank2 = low.shape[1]
    return pl.pallas_call(
        lambda *refs: attend_kernel(head, *refs),
        in_specs=[pl.BlockSpec(memory_space=pltpu.SMEM)] + [vmem] * 4,
        out_specs=[vmem] * 3,
        out_shape=[
            jax.ShapeDtypeStruct((seq, q_cols), BF16),
            jax.ShapeDtypeStruct((rank2, seq), BF16),
            jax.ShapeDtypeStruct((rank2 // 2, q_cols + 2 * head), BF16),
        ],
        compiler_params=params(),
        name="attend",
    )(scalars, mine, other, low, up)


def term_kernel(mid, up_sum, tok, out):
    rows = mid.shape[0]
    for i in range(out.shape[0]):
        width = out.shape[2]
        out[i, :rows, :] = dot(mid[...], tok[:, i * width : (i + 1) * width]).astype(BF16)
        out[i, rows:, :] = up_sum[...]


def term(mid, up_sum, tokens, parts):
    seq, width = tokens.shape
    per = 8
    shard = width // parts
    rows = mid.shape[0] + up_sum.shape[0]
    return pl.pallas_call(
        term_kernel,
        grid=(parts // per,),
        in_specs=[
            pl.BlockSpec(mid.shape, lambda k: (0, 0)),
            pl.BlockSpec(up_sum.shape, lambda k: (0, 0)),
            pl.BlockSpec((seq, per * shard), lambda k: (0, k)),
        ],
        out_specs=pl.BlockSpec((per, rows, shard), lambda k: (k, 0, 0)),
        out_shape=jax.ShapeDtypeStruct((parts, rows, shard), BF16),
        compiler_params=params(),
        name="term",
    )(mid, up_sum, tokens)


def output_kernel(where, context, own, flipped, their_own, their_flipped, out):
    half = own.shape[1]
    for core in range(2):
        for x_hi in range(2):

            @pl.when((where[0] == core) & (where[2] == x_hi))
            def _():
                shards = [(own, their_own), (flipped, their_flipped)]
                for x in range(2):
                    mine, theirs = shards[x ^ x_hi]
                    two = (mine, theirs) if core == 0 else (theirs, mine)
                    w = jnp.concatenate([h[0] for h in two], axis=1)
                    out[:, 2 * x * half : 2 * (x + 1) * half] = dot(context[...], w).astype(BF16)


def output_of(where, context, own, flipped, their_own, their_flipped, cost):
    seq, cols = context.shape
    count, rows, half = own.shape

    def late_of(k):
        return jnp.where(k < 8, k // 4, 5 - k // 4)

    def partner(k):
        early, late = k % 4, late_of(k)
        return jnp.where(early < 2, early, 5 - early) * 4 + late

    mine = pl.BlockSpec((1, rows, half), lambda k, w: (k, 0, 0))
    theirs = pl.BlockSpec((1, rows, half), lambda k, w: (partner(k), 0, 0))
    return pl.pallas_call(
        output_kernel,
        grid_spec=pltpu.PrefetchScalarGridSpec(
            num_scalar_prefetch=1,
            grid=(count,),
            in_specs=[pl.BlockSpec((seq, cols), lambda k, w: (0, 0)), mine, mine, theirs, theirs],
            out_specs=pl.BlockSpec((seq, 4 * half), lambda k, w: (0, place(w, k % 4, late_of(k)))),
        ),
        out_shape=jax.ShapeDtypeStruct((seq, count * 4 * half), BF16),
        compiler_params=params(),
        cost_estimate=cost,
        name="output",
    )(where, context, own, flipped, their_own, their_flipped)


def total_kernel(got, down, up):
    rows = down.shape[1]
    cols = up.shape[2]
    sums = [jnp.zeros(got.shape[1:], F32) for _ in range(2)]
    for f in range(got.shape[0]):
        part = got[f].astype(F32)
        one = part[rows : rows + 1, cols : cols + 1]
        sums[0] += part * (1.0 - one)
        sums[1] += part * one
    for s in range(2):
        down[s] = sums[s][:rows]
        up[s] = sums[s][rows:, :cols]


def total(got, rows, cols):
    parts, every, shard = got.shape
    vmem = pl.BlockSpec(memory_space=pltpu.VMEM)
    return pl.pallas_call(
        total_kernel,
        in_specs=[vmem],
        out_specs=[vmem] * 2,
        out_shape=[
            jax.ShapeDtypeStruct((2, rows, shard), F32),
            jax.ShapeDtypeStruct((2, every - rows, cols), F32),
        ],
        compiler_params=params(),
        name="total",
    )(got)


def body(
    tokens,
    cotangent,
    w_query,
    w_key,
    w_value,
    w_output,
    adapter_down,
    adapter_up,
    tenant_slot,
    lengths,
):
    seq, width = tokens.shape
    q_cols = w_query.shape[1]
    head = w_key.shape[1]
    shard, slots, _, rank = adapter_down.shape
    tenants = lax.axis_size("tenant")
    parts = lax.axis_size("fsdp")
    tenant = lax.axis_index("tenant").astype(jnp.int32)
    slot = tenant_slot[0]

    place = lax.axis_index("fsdp").astype(jnp.int32)
    y, z, x_hi = place // (2 * Z), place // 2 % Z, place % 2
    core = tenant % 2

    def shift(array, hops, late):
        to = []
        for f in range(parts):
            for t in range(tenants):
                along_y = (t % 2 == 0) == late
                f_y = (f // (2 * Z) + hops * along_y) % Y
                f_z = (f // 2 + hops * (not along_y)) % Z
                to.append((f * tenants + t, ((f_y * Z + f_z) * 2 + f % 2) * tenants + t))
        return lax.ppermute(array, ("fsdp", "tenant"), to)

    def swap(array):
        return lax.ppermute(array, "tenant", [(t, t ^ 1) for t in range(tenants)])

    where = jnp.stack([core, slot, x_hi, y, z])
    down = adapter_down.reshape(shard, slots * 2 * rank).T
    piece = pack(where, w_query, w_key, w_value, down, w_output)
    flipped = lax.ppermute(piece, "fsdp", [(f, f ^ 1) for f in range(parts)])
    hops = (1, 3, 2)
    early = {j: shift(piece, j, False) for j in hops}
    mate_tok = swap(tokens)
    flipped, early, mate_tok = lax.optimization_barrier((flipped, early, mate_tok))
    early[0] = piece
    own = jnp.stack([early[j] for j in range(4)])
    own_ahead, own_behind = shift(own, 1, True), shift(own, -1, True)
    early_flipped = {j: shift(flipped, j, False) for j in hops}
    early_flipped, own_ahead, own_behind, cot_then = lax.optimization_barrier(
        (early_flipped, own_ahead, own_behind, cotangent)
    )
    mate_cot = swap(cot_then)
    early_flipped[0] = flipped
    flip = jnp.stack([early_flipped[j] for j in range(4)])
    flip_ahead, flip_behind = shift(flip, 1, True), shift(flip, -1, True)
    kept_shape = jax.ShapeDtypeStruct((parts // 2, q_cols, shard // 2), BF16)
    out_shape = [
        jax.ShapeDtypeStruct((2 * seq, 2 * (q_cols + head)), F32),
        jax.ShapeDtypeStruct((seq, 2 * rank), F32),
        kept_shape,
    ]

    def add(pieces, lates, flip, base, sums):
        return arrive(
            where, tokens, cotangent, mate_tok, mate_cot, pieces, lates, flip, base, sums, out_shape
        )

    def halves(array):
        return [(array, 0), (array, 1)]

    *sums, kept = add(halves(own), (0,), 0, 0, (None, None, None))
    own_far = shift(own_ahead[:2], 1, True), shift(own_behind[2:], -1, True)
    *sums, kept = add(halves(own_ahead) + halves(own_behind), (1, 3), 0, 2, (*sums, kept))
    *sums, kept_flip = add(halves(flip), (0,), 1, 0, (*sums, None))
    flip_ahead, flip_behind, sums = lax.optimization_barrier((flip_ahead, flip_behind, sums))
    flip_far = shift(flip_ahead[:2], 1, True), shift(flip_behind[2:], -1, True)
    *sums, kept_flip = add(halves(flip_ahead) + halves(flip_behind), (1, 3), 1, 2, (*sums, kept_flip))
    *sums, kept = add([(x, 0) for x in own_far], (2,), 0, 6, (*sums, kept))
    *sums, kept_flip = add([(x, 0) for x in flip_far], (2,), 1, 6, (*sums, kept_flip))
    summed, low = sums
    other = swap(summed[seq:])
    other, kept, kept_flip = lax.optimization_barrier((other, kept, kept_flip))
    theirs, their_flip = swap(kept), swap(kept_flip)

    up = lax.dynamic_index_in_dim(adapter_up, slot, 0, keepdims=False)
    at_query = jnp.arange(q_cols + head)[None, :] < q_cols
    up = jnp.concatenate(
        [jnp.where(at_query, up, 0), jnp.where(at_query, 0, up)], axis=0
    ).astype(BF16)
    scalars = jnp.stack([slot, lengths[0]])
    context, mid, up_sum = attend(scalars, summed, other, low, up, head)
    sent = term(mid, up_sum, tokens, parts)
    got = lax.all_to_all(sent, "fsdp", split_axis=0, concat_axis=0, tiled=True)
    cost = pl.CostEstimate(
        flops=2 * seq * q_cols * width, bytes_accessed=4 * seq * width, transcendentals=0
    )
    output = output_of(where, context, kept, kept_flip, theirs, their_flip, cost)
    got, output = lax.optimization_barrier((got, output))
    down_sum, grad_up = total(got, 2 * rank, q_cols + head)
    grad_down = down_sum.reshape(slots * 2 * rank, shard).T.reshape(shard, slots, 2, rank)
    return (output, grad_down, grad_up)


def solution(mesh):
    placed = (
        P(("fsdp", "tenant"), None),
        P(("fsdp", "tenant"), None),
        P("fsdp", None),
        P("fsdp", None),
        P("fsdp", None),
        P(None, "fsdp"),
        P("fsdp", "tenant", None, None),
        P("tenant", None, None),
        P(("fsdp", "tenant")),
        P(("fsdp", "tenant")),
    )
    return jax.shard_map(
        body,
        mesh=mesh,
        in_specs=placed,
        out_specs=(
            P(("fsdp", "tenant"), None),
            P("fsdp", "tenant", None, None),
            P("tenant", None, None),
        ),
        check_vma=False,
    )
```

```python
import functools

import jax
import jax.numpy as jnp
from jax import lax
from jax.experimental import pallas as pl
from jax.experimental.pallas import tpu as pltpu
from jax.sharding import PartitionSpec as P

ADAPTER_SCALE = 2.0
Y, Z = 4, 4
VMEM = 48 * 1024 * 1024
NT = (((1,), (1,)), ((), ()))
TN = (((0,), (0,)), ((), ()))
F32 = jnp.float32
BF16 = jnp.bfloat16


def dot(a, b, dims=(((1,), (0,)), ((), ()))):
    return lax.dot_general(a, b, dims, preferred_element_type=F32)


def params(**kw):
    return pltpu.CompilerParams(vmem_limit_bytes=VMEM, **kw)


def pack_kernel(where, w_query, w_key, w_value, down, w_output, out):
    head, low = w_key.shape[1], down.shape[0]
    half = out.shape[1]
    out[:half, :] = w_query[...]
    out[half : 2 * half, :head] = w_key[...]
    out[half : 2 * half, head:] = w_value[...]
    for h in range(2):
        out[2 * half + h * low : 2 * half + (h + 1) * low, :] = down[:, h * half : (h + 1) * half]
    out[2 * half + 2 * low :, :] = w_output[...]


def pack(where, w_query, w_key, w_value, down, w_output):
    half = w_query.shape[0] // 2
    q_cols, head, low = w_query.shape[1], w_key.shape[1], down.shape[0]
    rows = lambda cols: pl.BlockSpec((half, cols), lambda k, w: (w[0], 0))
    return pl.pallas_call(
        pack_kernel,
        grid_spec=pltpu.PrefetchScalarGridSpec(
            num_scalar_prefetch=1,
            grid=(1,),
            in_specs=[
                rows(q_cols),
                rows(head),
                rows(head),
                pl.BlockSpec(down.shape, lambda k, w: (0, 0)),
                pl.BlockSpec((q_cols, half), lambda k, w: (0, w[0])),
            ],
            out_specs=pl.BlockSpec((3 * half + 2 * low, half), lambda k, w: (0, 0)),
        ),
        out_shape=jax.ShapeDtypeStruct((3 * half + 2 * low, half), BF16),
        compiler_params=pltpu.CompilerParams(vmem_limit_bytes=56 * 1024 * 1024),
        name="pack",
    )(where, w_query, w_key, w_value, down, w_output)


def arrive_kernel(where, *refs, pieces, fresh):
    tok, cot, mate_tok, mate_cot = refs[0:2], refs[2:4], refs[4:6], refs[6:8]
    arrived, refs = refs[8 : 8 + pieces], refs[8 + pieces :]
    both, low, kept = refs[-3:]
    step = pl.program_id(0)

    if fresh:

        @pl.when(step == 0)
        def _():
            for new in (both, low):
                new[...] = jnp.zeros_like(new)

    core, slot = where[0], where[1]
    half = arrived[0].shape[2]
    first = arrived[0].shape[1] - half

    def add(shard):
        side = pl.multiple_of(core * half, half)
        rows = jnp.concatenate(
            [
                jnp.concatenate([t[:, pl.ds(side, half)] for t in tok], axis=1),
                jnp.concatenate([t[...] for t in mate_tok], axis=1),
            ],
            axis=0,
        )
        for g in range(2):
            cols = slice(g * half, (g + 1) * half)
            both[:, cols] += dot(rows, jnp.concatenate([shard[i, cols, :] for i in range(2)], axis=0))
        rows = jnp.concatenate([jnp.concatenate([t[...] for t in two], axis=1) for two in (cot, mate_cot)], axis=0)
        w = jnp.concatenate([shard[i, first:, :] for i in range(2)], axis=1)
        both[:, 2 * half :] += dot(rows, w, NT)
        kept[...] = shard[:, first:, :]
        down = [
            shard[i, pl.ds(pl.multiple_of(2 * half + h * 64 + slot * 32, 32), 32), :]
            for i in range(2)
            for h in range(2)
        ]
        rows = jnp.concatenate([t[...] for t in tok], axis=1)
        low[...] += dot(rows, jnp.concatenate(down, axis=1), NT)

    for i in range(pieces):

        @pl.when(step == i)
        def _():
            add(arrived[i])


def place(w, early, late):
    y = (w[3] - jnp.where(w[0] == 0, late, early) + Y) % Y
    z = (w[4] - jnp.where(w[0] == 0, early, late) + Z) % Z
    return y * Z + z


def arrive(where, tokens, cotangent, mate_tok, mate_cot, pieces, lates, flip, base, sums, out_shape):
    seq = tokens.shape[0]
    rows, half = pieces[0][0].shape[1:]

    def at(k, w, p):
        late = jnp.int32(lates[0])
        for i in range(1, len(lates)):
            late = jnp.where(k >= 2 * i, lates[i], late)
        return 2 * place(w, 2 * (k % 2) + p, late) + (w[2] ^ flip)

    def two(cols, index):
        return [pl.BlockSpec((seq, cols), lambda k, w, p=p: (0, index(k, w, p))) for p in range(2)]

    core_half = lambda k, w, p: 2 * at(k, w, p) + w[0]
    whole = [pl.BlockSpec(memory_space=pltpu.VMEM)] * 2
    fresh = [x is None for x in sums]
    given = [x for x in sums if x is not None]
    inputs = [tokens] * 2 + [cotangent] * 2 + [mate_tok] * 2 + [mate_cot] * 2 + [a for a, _ in pieces]
    kept_at = [i for i in range(3) if not fresh[i]]
    kept_spec = [] if fresh[2] else [pl.BlockSpec(memory_space=pl.ANY)]
    return pl.pallas_call(
        functools.partial(arrive_kernel, pieces=len(pieces), fresh=fresh[0]),
        grid_spec=pltpu.PrefetchScalarGridSpec(
            num_scalar_prefetch=1,
            grid=(len(pieces),),
            in_specs=two(2 * half, at)
            + two(half, core_half) * 3
            + [pl.BlockSpec((2, rows, half), lambda k, w, i=i: (i, 0, 0)) for _, i in pieces]
            + ([] if fresh[0] else whole)
            + kept_spec,
            out_specs=whole + [pl.BlockSpec((2, half, half), lambda k, w: (base + k, 0, 0))],
        ),
        out_shape=out_shape,
        input_output_aliases=dict(zip(range(1 + len(inputs), 1 + len(inputs) + len(given)), kept_at)),
        compiler_params=params(),
        cost_estimate=pl.CostEstimate(flops=len(pieces) * 2**29, bytes_accessed=len(pieces) * 2**21, transcendentals=0),
        name="arrive",
    )(where, *inputs, *given)


def attend_kernel(head, scalars, mine, other, low_in, up, context, mid, up_sum):
    seq, total = other.shape
    q_cols = (total - 2 * head) // 2
    heads = q_cols // head
    length = scalars[1]
    inv_root = 1.0 / jnp.sqrt(F32(head))
    low = low_in[...].astype(BF16)
    added = ADAPTER_SCALE * dot(low, up[...])
    summed = mine[:seq, :] + other[...]
    qkv, dctx = summed[:, : total - q_cols], summed[:, total - q_cols :]
    query = (qkv[:, :q_cols] + added[:, :q_cols]).astype(BF16)
    key = qkv[:, q_cols : q_cols + head].astype(BF16)
    value = (qkv[:, q_cols + head :] + added[:, q_cols:]).astype(BF16)
    row = lax.broadcasted_iota(jnp.int32, (seq, seq), 0)
    col = lax.broadcasted_iota(jnp.int32, (seq, seq), 1)
    mask = (col <= row) & (col < length)
    keep = lax.broadcasted_iota(jnp.int32, (seq, q_cols), 0) < length
    dctx = jnp.where(keep, dctx, 0.0).astype(BF16)
    d_value = jnp.zeros((seq, head), F32)
    outs, dqs = [], []
    for h in range(heads):
        cols = slice(h * head, (h + 1) * head)
        scores = dot(query[:, cols], key, NT) * inv_root
        scores = jnp.where(mask, scores, F32(-1e30))
        top = jnp.max(scores, axis=1, keepdims=True)
        expo = jnp.where(mask, jnp.exp(scores - top), 0.0)
        probs = expo / jnp.sum(expo, axis=1, keepdims=True)
        probs_b = probs.astype(BF16)
        outs.append(dot(probs_b, value))
        d_head = dctx[:, cols]
        d_probs = dot(d_head, value, NT)
        d_value += dot(probs_b, d_head, TN)
        delta = jnp.sum(probs * d_probs, axis=1, keepdims=True)
        d_scores = (probs * (d_probs - delta)).astype(BF16)
        dqs.append(dot(d_scores, key) * inv_root)
    context[...] = jnp.where(keep, jnp.concatenate(outs, axis=1), 0.0).astype(BF16)
    d_all = jnp.concatenate(dqs + [d_value], axis=1).astype(BF16)
    mid[...] = (ADAPTER_SCALE * dot(up[...], d_all, NT)).astype(BF16)
    sums = ADAPTER_SCALE * dot(low, d_all, TN)
    rank = sums.shape[0] // 2
    slot = jnp.full((rank, head), scalars[0], jnp.int32).astype(F32)
    up_sum[...] = jnp.concatenate([sums[:rank, :q_cols], sums[rank:, q_cols:], slot], axis=1).astype(BF16)


def attend(scalars, mine, other, low, up, head):
    seq, total = other.shape
    q_cols = (total - 2 * head) // 2
    vmem = pl.BlockSpec(memory_space=pltpu.VMEM)
    rank2 = low.shape[1]
    return pl.pallas_call(
        lambda *refs: attend_kernel(head, *refs),
        in_specs=[pl.BlockSpec(memory_space=pltpu.SMEM)] + [vmem] * 4,
        out_specs=[vmem] * 3,
        out_shape=[
            jax.ShapeDtypeStruct((seq, q_cols), BF16),
            jax.ShapeDtypeStruct((rank2, seq), BF16),
            jax.ShapeDtypeStruct((rank2 // 2, q_cols + 2 * head), BF16),
        ],
        compiler_params=params(),
        name="attend",
    )(scalars, mine, other, low, up)


def term_kernel(mid, up_sum, tok, out):
    rows = mid.shape[0]
    for i in range(out.shape[0]):
        width = out.shape[2]
        out[i, :rows, :] = dot(mid[...], tok[:, i * width : (i + 1) * width]).astype(BF16)
        out[i, rows:, :] = up_sum[...]


def term(mid, up_sum, tokens, parts):
    seq, width = tokens.shape
    per = 8
    shard = width // parts
    rows = mid.shape[0] + up_sum.shape[0]
    return pl.pallas_call(
        term_kernel,
        grid=(parts // per,),
        in_specs=[
            pl.BlockSpec(mid.shape, lambda k: (0, 0)),
            pl.BlockSpec(up_sum.shape, lambda k: (0, 0)),
            pl.BlockSpec((seq, per * shard), lambda k: (0, k)),
        ],
        out_specs=pl.BlockSpec((per, rows, shard), lambda k: (k, 0, 0)),
        out_shape=jax.ShapeDtypeStruct((parts, rows, shard), BF16),
        compiler_params=params(),
        name="term",
    )(mid, up_sum, tokens)


def output_kernel(where, context, own, flipped, their_own, their_flipped, out):
    half = own.shape[1]
    for core in range(2):
        for x_hi in range(2):

            @pl.when((where[0] == core) & (where[2] == x_hi))
            def _():
                shards = [(own, their_own), (flipped, their_flipped)]
                for x in range(2):
                    mine, theirs = shards[x ^ x_hi]
                    two = (mine, theirs) if core == 0 else (theirs, mine)
                    w = jnp.concatenate([h[0] for h in two], axis=1)
                    out[:, 2 * x * half : 2 * (x + 1) * half] = dot(context[...], w).astype(BF16)


def output_of(where, context, own, flipped, their_own, their_flipped, cost):
    seq, cols = context.shape
    count, rows, half = own.shape

    def late_of(k):
        return jnp.where(k < 8, k // 4, 5 - k // 4)

    def partner(k):
        early, late = k % 4, late_of(k)
        return jnp.where(early < 2, early, 5 - early) * 4 + late

    mine = pl.BlockSpec((1, rows, half), lambda k, w: (k, 0, 0))
    theirs = pl.BlockSpec((1, rows, half), lambda k, w: (partner(k), 0, 0))
    return pl.pallas_call(
        output_kernel,
        grid_spec=pltpu.PrefetchScalarGridSpec(
            num_scalar_prefetch=1,
            grid=(count,),
            in_specs=[pl.BlockSpec((seq, cols), lambda k, w: (0, 0)), mine, mine, theirs, theirs],
            out_specs=pl.BlockSpec((seq, 4 * half), lambda k, w: (0, place(w, k % 4, late_of(k)))),
        ),
        out_shape=jax.ShapeDtypeStruct((seq, count * 4 * half), BF16),
        compiler_params=params(),
        cost_estimate=cost,
        name="output",
    )(where, context, own, flipped, their_own, their_flipped)


def total_kernel(got, down, up):
    rows = down.shape[1]
    cols = up.shape[2]
    sums = [jnp.zeros(got.shape[1:], F32) for _ in range(2)]
    for f in range(got.shape[0]):
        part = got[f].astype(F32)
        one = part[rows : rows + 1, cols : cols + 1]
        sums[0] += part * (1.0 - one)
        sums[1] += part * one
    for s in range(2):
        down[s] = sums[s][:rows]
        up[s] = sums[s][rows:, :cols]


def total(got, rows, cols):
    parts, every, shard = got.shape
    vmem = pl.BlockSpec(memory_space=pltpu.VMEM)
    return pl.pallas_call(
        total_kernel,
        in_specs=[vmem],
        out_specs=[vmem] * 2,
        out_shape=[
            jax.ShapeDtypeStruct((2, rows, shard), F32),
            jax.ShapeDtypeStruct((2, every - rows, cols), F32),
        ],
        compiler_params=params(),
        name="total",
    )(got)


def body(
    tokens,
    cotangent,
    w_query,
    w_key,
    w_value,
    w_output,
    adapter_down,
    adapter_up,
    tenant_slot,
    lengths,
):
    seq, width = tokens.shape
    q_cols = w_query.shape[1]
    head = w_key.shape[1]
    shard, slots, _, rank = adapter_down.shape
    tenants = lax.axis_size("tenant")
    parts = lax.axis_size("fsdp")
    tenant = lax.axis_index("tenant").astype(jnp.int32)
    slot = tenant_slot[0]

    place = lax.axis_index("fsdp").astype(jnp.int32)
    y, z, x_hi = place // (2 * Z), place // 2 % Z, place % 2
    core = tenant % 2

    def shift(array, hops, late):
        to = []
        for f in range(parts):
            for t in range(tenants):
                along_y = (t % 2 == 0) == late
                f_y = (f // (2 * Z) + hops * along_y) % Y
                f_z = (f // 2 + hops * (not along_y)) % Z
                to.append((f * tenants + t, ((f_y * Z + f_z) * 2 + f % 2) * tenants + t))
        return lax.ppermute(array, ("fsdp", "tenant"), to)

    def swap(array):
        return lax.ppermute(array, "tenant", [(t, t ^ 1) for t in range(tenants)])

    where = jnp.stack([core, slot, x_hi, y, z])
    down = adapter_down.reshape(shard, slots * 2 * rank).T
    piece = pack(where, w_query, w_key, w_value, down, w_output)
    flipped = lax.ppermute(piece, "fsdp", [(f, f ^ 1) for f in range(parts)])
    hops = (1, 3, 2)
    early = {j: shift(piece, j, False) for j in hops}
    mate_tok = swap(tokens)
    flipped, early, mate_tok = lax.optimization_barrier((flipped, early, mate_tok))
    early[0] = piece
    own = jnp.stack([early[j] for j in range(4)])
    own_ahead, own_behind = shift(own, 1, True), shift(own, -1, True)
    early_flipped = {j: shift(flipped, j, False) for j in hops}
    early_flipped, own_ahead, own_behind, cot_then = lax.optimization_barrier(
        (early_flipped, own_ahead, own_behind, cotangent)
    )
    mate_cot = swap(cot_then)
    early_flipped[0] = flipped
    flip = jnp.stack([early_flipped[j] for j in range(4)])
    flip_ahead, flip_behind = shift(flip, 1, True), shift(flip, -1, True)
    kept_shape = jax.ShapeDtypeStruct((parts // 2, q_cols, shard // 2), BF16)
    out_shape = [
        jax.ShapeDtypeStruct((2 * seq, 2 * (q_cols + head)), F32),
        jax.ShapeDtypeStruct((seq, 2 * rank), F32),
        kept_shape,
    ]

    def add(pieces, lates, flip, base, sums):
        return arrive(
            where, tokens, cotangent, mate_tok, mate_cot, pieces, lates, flip, base, sums, out_shape
        )

    def halves(array):
        return [(array, 0), (array, 1)]

    own_far = shift(own_ahead[:2], 1, True), shift(own_behind[2:], -1, True)
    here = halves(own) + halves(own_ahead) + halves(own_behind)
    *sums, kept = add(here, (0, 1, 3), 0, 0, (None, None, None))
    *sums, kept_flip = add(halves(flip), (0,), 1, 0, (*sums, None))
    flip_ahead, flip_behind, sums = lax.optimization_barrier((flip_ahead, flip_behind, sums))
    flip_far = shift(flip_ahead[:2], 1, True), shift(flip_behind[2:], -1, True)
    *sums, kept_flip = add(halves(flip_ahead) + halves(flip_behind), (1, 3), 1, 2, (*sums, kept_flip))
    *sums, kept = add([(x, 0) for x in own_far], (2,), 0, 6, (*sums, kept))
    *sums, kept_flip = add([(x, 0) for x in flip_far], (2,), 1, 6, (*sums, kept_flip))
    summed, low = sums
    other = swap(summed[seq:])
    other, kept, kept_flip = lax.optimization_barrier((other, kept, kept_flip))
    theirs, their_flip = swap(kept), swap(kept_flip)

    up = lax.dynamic_index_in_dim(adapter_up, slot, 0, keepdims=False)
    at_query = jnp.arange(q_cols + head)[None, :] < q_cols
    up = jnp.concatenate(
        [jnp.where(at_query, up, 0), jnp.where(at_query, 0, up)], axis=0
    ).astype(BF16)
    scalars = jnp.stack([slot, lengths[0]])
    context, mid, up_sum = attend(scalars, summed, other, low, up, head)
    sent = term(mid, up_sum, tokens, parts)
    got = lax.all_to_all(sent, "fsdp", split_axis=0, concat_axis=0, tiled=True)
    cost = pl.CostEstimate(
        flops=2 * seq * q_cols * width, bytes_accessed=4 * seq * width, transcendentals=0
    )
    output = output_of(where, context, kept, kept_flip, theirs, their_flip, cost)
    got, output = lax.optimization_barrier((got, output))
    down_sum, grad_up = total(got, 2 * rank, q_cols + head)
    grad_down = down_sum.reshape(slots * 2 * rank, shard).T.reshape(shard, slots, 2, rank)
    return (output, grad_down, grad_up)


def solution(mesh):
    placed = (
        P(("fsdp", "tenant"), None),
        P(("fsdp", "tenant"), None),
        P("fsdp", None),
        P("fsdp", None),
        P("fsdp", None),
        P(None, "fsdp"),
        P("fsdp", "tenant", None, None),
        P("tenant", None, None),
        P(("fsdp", "tenant")),
        P(("fsdp", "tenant")),
    )
    return jax.shard_map(
        body,
        mesh=mesh,
        in_specs=placed,
        out_specs=(
            P(("fsdp", "tenant"), None),
            P("fsdp", "tenant", None, None),
            P("tenant", None, None),
        ),
        check_vma=False,
    )
```
